256 devices in a mesh: seq: 64 (over x_lo, z, y), head: 4 (over x_hi, core).
Axes of the slice: x: 4 (x_hi: 2, x_lo: 2; x = x_hi * 2 + x_lo), y: 4, z: 8, core: 2. Of those that a mesh axis runs over, the one named last changes fastest.
Arguments:
- level_input: bfloat16 [32768, 1536], P('seq', 'head'), may hold values from -6 to 6
- norm_gain: float32 [1536], replicated, may hold values from 0.1 to 1.9
- query_weight: bfloat16 [1536, 1024], P(None, 'head'), may hold values from -0.15625 to 0.15625
- key_weight: bfloat16 [1536, 128], replicated, may hold values from -0.15625 to 0.15625
- value_weight: bfloat16 [1536, 192], replicated, may hold values from -0.15625 to 0.15625
- out_weight: bfloat16 [1536, 1536], P('head'), may hold values from -0.15625 to 0.15625
- up_weight: bfloat16 [5, 1536, 1536], P(None, None, 'head'), may hold values from -0.0625 to 0.0625
- grad_output: bfloat16 [32768, 1536], P('seq', 'head'), may hold values from -6 to 6
Outputs:
- level_output: bfloat16 [32768, 1536], P('seq', 'head')
- grad_mixed: bfloat16 [16384, 1536], P('seq', 'head')
The draws below stay inside these ranges and needn't reach their ends.
All inputs are finite; a program needn't handle non-finite values.
Results may differ from the reference program's by a relative error of at most 0.015.
Values may be sent and summed in bfloat16 or wider, within the bound.
A program may use at most 128 MiB of HBM per device.

```python
import jax
import jax.numpy as jnp
from jax import lax

F = 1536
H = 8
DK = 128
DV = 192
KW = 5
ROWS = 512
TOTAL = 32768


def shard_levels(rng, dims, split, smallest, largest):
    loudness, own = 1.0, jax.random.fold_in(rng, 6)
    for axis_at, shards_of in split:
        heights = jnp.exp(jax.random.uniform(jax.random.fold_in(own, axis_at), (shards_of,), jnp.float32, smallest / len(split), largest / len(split)))
        loudness = loudness * jnp.repeat(heights, dims[axis_at] // shards_of).reshape([-1 if axis == axis_at else 1 for axis in range(len(dims))])
    return loudness


def noise(key, dims, width, most, split=(), held_as=jnp.bfloat16):
    loudness = shard_levels(key, dims, split, -0.22, 0.18) if split else 1.0
    entries = jax.random.normal(key, dims, jnp.float32) * width * loudness
    return jnp.minimum(jnp.maximum(entries, -most), most).astype(held_as)


def setup_inputs(seed: int = 0) -> dict:
    key_list = jax.random.split(jax.random.key(seed), 9)
    level_input = noise(key_list[0], (TOTAL, F), 1.0, 6.0, ((0, 64), (1, 4)))
    norm_gain = jnp.clip(1.0 + 0.18 * jax.random.normal(key_list[1], (F,), jnp.float32), 0.1, 1.9)
    query_weight = noise(key_list[2], (F, H * DK), F ** -0.5, 0.15625, ((1, 4),))
    key_weight = noise(key_list[3], (F, DK), F ** -0.5, 0.15625)
    value_weight = noise(key_list[4], (F, DV), F ** -0.5, 0.15625)
    out_weight = noise(key_list[5], (H * DV, F), (H * DV) ** -0.5, 0.15625, ((0, 4),))
    up_weight = noise(key_list[6], (KW, F, F), (KW * F) ** -0.5, 0.0625, ((2, 4),))
    grad_output = noise(key_list[7], (TOTAL, F), 1.0, 6.0, ((0, 64), (1, 4)))
    return {"level_input": level_input, "norm_gain": norm_gain, "query_weight": query_weight, "key_weight": key_weight, "value_weight": value_weight, "out_weight": out_weight, "up_weight": up_weight, "grad_output": grad_output}


score_scale = 24.0
epsilon = 1e-06

def rms_normalize(values):
    return values * lax.rsqrt(lax.optimization_barrier(jnp.mean(values * values, axis=-1, keepdims=True)) + epsilon)

def contract_last(left, right):
    return lax.dot_general(left, right, (((1,), (1,)), ((), ())), preferred_element_type=jnp.float32)

def reference(level_input, norm_gain, query_weight, key_weight, value_weight, out_weight, up_weight, grad_output):
    total_rows = level_input.shape[0]
    half_rows = total_rows // 2
    input_float = level_input.astype(jnp.float32)
    pooled = (0.5 * (input_float[0::2] + input_float[1::2])).astype(jnp.bfloat16)
    pooled_float = pooled.astype(jnp.float32)
    normed = (rms_normalize(pooled_float) * norm_gain).astype(jnp.bfloat16)
    queries = jnp.dot(normed, query_weight, preferred_element_type=jnp.float32)
    queries = rms_normalize(queries.reshape(half_rows, H, DK)).astype(jnp.bfloat16)
    keys_all = rms_normalize(jnp.dot(normed, key_weight, preferred_element_type=jnp.float32)).astype(jnp.bfloat16)
    values_all = jnp.dot(normed, value_weight, preferred_element_type=jnp.float32).astype(jnp.bfloat16)
    block_rows = ROWS // 2

    def attend(query_block):
        flat = query_block.reshape(block_rows * H, DK)
        scores = contract_last(flat, keys_all) * (score_scale / DK)
        weights_exp = jnp.exp(scores)
        denominator = lax.optimization_barrier(jnp.sum(weights_exp, axis=1, keepdims=True))
        numerator = jnp.dot(weights_exp.astype(jnp.bfloat16), values_all, preferred_element_type=jnp.float32)
        return (numerator / denominator).astype(jnp.bfloat16).reshape(block_rows, H * DV)
    attended = lax.map(attend, queries.reshape(half_rows // block_rows, block_rows, H, DK))
    attended = attended.reshape(half_rows, H * DV)
    mixed = (pooled_float + jnp.dot(attended, out_weight, preferred_element_type=jnp.float32)).astype(jnp.bfloat16)
    upsampled = jnp.repeat(mixed, 2, axis=0)
    padded = jnp.pad(upsampled, ((2, 2), (0, 0)))
    convolved = jnp.zeros((total_rows, up_weight.shape[2]), jnp.float32)
    for tap in range(KW):
        convolved = convolved + jnp.dot(padded[tap:tap + total_rows], up_weight[tap], preferred_element_type=jnp.float32)
    level_output = (input_float + convolved).astype(jnp.bfloat16)
    padded_grad = jnp.pad(grad_output, ((2, 2), (0, 0)))
    grad_upsampled = jnp.zeros((total_rows, up_weight.shape[1]), jnp.float32)
    for tap in range(KW):
        grad_upsampled = grad_upsampled + contract_last(padded_grad[4 - tap:4 - tap + total_rows], up_weight[tap])
    grad_mixed = (grad_upsampled[0::2] + grad_upsampled[1::2]).astype(jnp.bfloat16)
    return (level_output, grad_mixed)
```

```python
import functools

import jax
import jax.numpy as jnp
from jax import lax
from jax.experimental import pallas as pl
from jax.experimental.pallas import tpu as pltpu
from jax.sharding import PartitionSpec as P

MESH = pl.DeviceIdType.MESH
F32, BF16 = jnp.float32, jnp.bfloat16
EPS = 1e-06
QSCALE = 24.0 / 128.0 * 1.4426950408889634
N_SEM = 64


def nt_dot(a, b):
    return lax.dot_general(a, b, (((1,), (1,)), ((), ())), preferred_element_type=F32)


def nn_dot(a, b):
    return jnp.dot(a, b, preferred_element_type=F32)


def rms(v):
    return v * lax.rsqrt(jnp.mean(v * v, axis=-1, keepdims=True) + EPS)


def fill(wide, narrow):
    for c in range(3):
        wide[c] = narrow[:, c * 128 : (c + 1) * 128].astype(F32)


def strided(wide, start):
    return jnp.concatenate([wide[c, pl.ds(start, 256, stride=2), :] for c in range(3)], axis=1)


def kernel(
    level_hbm, gain_hbm, wq_hbm, wk_hbm, wv_hbm, wo_hbm, up_hbm, grad_hbm,
    out_ref, gm_ref,
    lv, gain, wq, wk, wv, wo, up, gbuf,
    lv32, g32, xbuf, normed, qall, kva, kvb, acc,
    gm_own, gm_send, gm_recv, o_send, o_recv, r_own, r_send, r_recv,
    mbuf, halo, tbuf, o32,
    load_sem, send_sem, recv_sem,
):
    s = lax.axis_index("seq")
    h = lax.axis_index("head")
    xl, z, y = s // 32, (s // 4) % 8, s % 4

    def at(xl_, z_, y_):
        return ((xl_ * 8 + z_) * 4 + y_, h)

    X = at(1 - xl, z, y)
    ZP, ZM = at(xl, (z + 1) % 8, y), at(xl, (z + 7) % 8, y)
    YP, YM = at(xl, z, (y + 1) % 4), at(xl, z, (y + 3) % 4)
    peers = [(s, (h + j) % 4) for j in (1, 2, 3)]
    nxt, prv = (s + 1) % 64, (s + 63) % 64

    loads = []

    def load(src, dst):
        c = pltpu.make_async_copy(src, dst, load_sem.at[len(loads)])
        c.start()
        loads.append(c)
        return c

    l_lv = load(level_hbm, lv)
    l_g = load(grad_hbm, gbuf.at[pl.ds(16, 512)])
    l_gain = load(gain_hbm, gain)
    l_wk = load(wk_hbm, wk)
    l_wv = load(wv_hbm, wv)
    l_wq = load(wq_hbm, wq)
    l_up = load(up_hbm, up)
    l_wo = load(wo_hbm, wo)

    bar = pltpu.get_barrier_semaphore()
    friends = [X, ZP, ZM, YP, YM] + peers
    friends += [(q, hh) for q in (nxt, prv) for hh in range(4)]
    for f in friends:
        pl.semaphore_signal(bar, inc=1, device_id=f, device_id_type=MESH)

    count = [0]
    sent = []

    def remote(src, dst, dev):
        i = count[0]
        count[0] += 1
        return pltpu.make_async_remote_copy(
            src_ref=src, dst_ref=dst, send_sem=send_sem.at[i], recv_sem=recv_sem.at[i],
            device_id=dev, device_id_type=MESH,
        )

    def send(src, dst, dev):
        c = remote(src, dst, dev)
        c.start()
        sent.append(c)
        return c

    l_lv.wait()
    fill(lv32, lv)
    pooled = 0.5 * (strided(lv32, 0) + strided(lv32, 1))
    xbuf[h] = pooled.astype(BF16)
    l_g.wait()
    pl.semaphore_wait(bar, len(friends))

    c_x = [send(xbuf.at[h], xbuf.at[h], p) for p in peers]
    c_g = [
        send(gbuf.at[pl.ds(512, 16)], gbuf.at[pl.ds(0, 16)], (nxt, h)),
        send(gbuf.at[pl.ds(16, 16)], gbuf.at[pl.ds(528, 16)], (prv, h)),
    ]

    for c in c_g:
        c.wait_recv()
    fill(g32, gbuf)

    @pl.when(s == 0)
    def _():
        g32[:, 0:16, :] = jnp.zeros((3, 16, 128), F32)

    @pl.when(s == 63)
    def _():
        g32[:, 528:544, :] = jnp.zeros((3, 16, 128), F32)

    rows = [strided(g32, 16 + d) for d in range(-2, 4)]
    pair = [(rows[4 - t] + rows[5 - t]).astype(BF16) for t in range(5)]
    l_up.wait()
    for j in (1, 2, 3, 0):
        p = (h + j) % 4
        part = sum(nt_dot(pair[t], up[t, pl.ds(p * 384, 384), :]) for t in range(5))
        if j:
            gm_send[j - 1] = part.astype(BF16)
        else:
            gm_own[...] = part

    for c in c_x:
        c.wait_recv()
    l_gain.wait()
    xs = [xbuf[c].astype(F32) for c in range(4)]
    sq = sum(jnp.sum(v * v, axis=-1, keepdims=True) for v in xs)
    inv = lax.rsqrt(sq / 1536.0 + EPS)
    for c in range(4):
        sl = slice(c * 384, (c + 1) * 384)
        normed[:, sl] = (xs[c] * inv * gain[0:1, sl]).astype(BF16)

    l_wk.wait()
    l_wv.wait()
    mine = normed[pl.ds(pl.multiple_of(h * 64, 64), 64), :]
    kk = rms(nn_dot(mine, wk[...])).astype(BF16)
    vv = nn_dot(mine, wv[...]).astype(BF16)
    one = (lax.broadcasted_iota(jnp.int32, (64, 64), 1) == 0).astype(BF16)
    kv = jnp.concatenate([kk, vv, one], axis=1)

    def sa(xl_, z_, y_):
        return pl.multiple_of(((y_ * 8 + z_) * 2 + xl_) * 32, 32)

    def sb(xl_, z_, y_):
        return pl.multiple_of(((z_ * 4 + y_) * 2 + xl_) * 32, 32)

    def a_rows(start, n):
        return kva.at[pl.ds(start, n)]

    def b_rows(start, n):
        return kvb.at[pl.ds(start, n)]

    own_a, own_b = sa(xl, z, y), sb(xl, z, y)
    kva[pl.ds(own_a, 32), :] = kv[0:32]
    kvb[pl.ds(own_b, 32), :] = kv[32:64]
    c_xa = send(a_rows(own_a, 32), a_rows(own_a, 32), X)
    c_xb = send(b_rows(own_b, 32), b_rows(own_b, 32), X)

    l_wq.wait()
    q = nn_dot(normed[...], wq[...])
    own_q = pl.multiple_of(h * 512, 512)
    for i in range(2):
        qn = rms(q[:, i * 128 : (i + 1) * 128]) * QSCALE
        qall[pl.ds(own_q + i * 256, 256), :] = qn.astype(BF16)
    c_q = [send(qall.at[pl.ds(own_q, 512)], qall.at[pl.ds(own_q, 512)], p) for p in peers]

    def a_pair(z_):
        return a_rows(sa(0, (z_ + 16) % 8, y), 64)

    def b_pair():
        return b_rows(sb(0, z, y), 64)

    def b_group(z_):
        return b_rows(sb(0, (z_ + 16) % 8, 0), 256)

    c_xb.wait_recv()
    c_by = [send(b_pair(), b_pair(), YP), send(b_pair(), b_pair(), YM)]
    c_xa.wait_recv()
    c_ap, c_am = [send(a_pair(z), a_pair(z), ZP)], [send(a_pair(z), a_pair(z), ZM)]
    c_by[0].wait_recv()
    left = b_rows(sb(0, z, (y + 3) % 4), 64)
    c_by2 = send(left, left, YP)
    c_by[1].wait_recv()
    for k in (1, 2, 3):
        c_ap[-1].wait_recv()
        c_ap.append(send(a_pair(z - k), a_pair(z - k), ZP))
        c_am[-1].wait_recv()
        if k < 3:
            c_am.append(send(a_pair(z + k), a_pair(z + k), ZM))
        if k == 1:
            c_by2.wait_recv()
            bp = [remote(b_group(z - i), b_group(z - i), ZP) for i in range(3)]
            bm = [remote(b_group(z + i), b_group(z + i), ZM) for i in range(4)]
            bp[0].start()
            bm[0].start()
    c_ap[-1].wait_recv()

    def a_half(y_, half):
        return a_rows(pl.multiple_of(((y_ + 8) % 4) * 512 + half * 256, 256), 256)

    ar = [remote(a_half(y, i), a_half(y, i), YP) for i in range(2)]
    al = [remote(a_half(y, i), a_half(y, i), YM) for i in range(2)]
    a2r = remote(a_half(y - 1, 0), a_half(y - 1, 0), YP)
    a2l = remote(a_half(y + 1, 1), a_half(y + 1, 1), YM)
    ar[0].start()
    al[1].start()
    ar[1].start()
    al[0].start()
    c_gm = [remote(gm_send.at[j], gm_recv.at[j], peers[j]) for j in range(3)]
    for c in c_q:
        c.wait_recv()
    for c in c_gm:
        c.start()
    acc[...] = jnp.zeros_like(acc)

    @pl.loop(0, 4)
    def _(i):
        @pl.when(i == 0)
        def _():
            bm[0].wait_recv()
            bm[1].start()

        @pl.when(i == 1)
        def _():
            bp[0].wait_recv()
            bp[1].start()
            bm[1].wait_recv()
            bm[2].start()
            al[1].wait_recv()
            a2l.start()
            ar[0].wait_recv()
            a2r.start()
            al[0].wait_recv()

        @pl.when(i == 2)
        def _():
            bp[1].wait_recv()
            bp[2].start()
            bm[2].wait_recv()
            bm[3].start()
            ar[1].wait_recv()

        @pl.when(i == 3)
        def _():
            bp[2].wait_recv()
            bm[3].wait_recv()
            a2r.wait_recv()
            a2l.wait_recv()

        ya = (y + i + i // 2 - 2 * (i // 3)) % 4
        oa = pl.multiple_of(ya * 512, 512)
        ob0 = pl.multiple_of(((z - i + 8) % 8) * 256, 256)
        ob1 = pl.multiple_of(((z + i + 1) % 8) * 256, 256)
        ka = jnp.concatenate(
            [kva[pl.ds(oa, 512), :], kvb[pl.ds(ob0, 256), :], kvb[pl.ds(ob1, 256), :]], axis=0
        )
        keys, vals = ka[:, 0:128], ka[:, 128:384]
        for qi in range(4):
            rs = slice(qi * 512, (qi + 1) * 512)
            w = jnp.exp2(nt_dot(qall[rs, :], keys)).astype(BF16)
            acc[rs, :] += nn_dot(w, vals)

    lane = lax.broadcasted_iota(jnp.int32, (512, 256), 1)
    c_o = []
    for j in (1, 2, 3):
        p = (h + j) % 4
        part = acc[pl.ds(pl.multiple_of(p * 512, 512), 512), :]
        den = part[:, 192:193]
        low = den - den.astype(BF16).astype(F32)
        o_send[j - 1] = jnp.where(lane == 193, low, part).astype(BF16)
        c_o.append(send(o_send.at[j - 1], o_recv.at[j - 1], peers[j - 1]))

    for c in c_gm:
        c.wait_recv()
    gm = gm_own[...]
    for j in range(3):
        gm = gm + gm_recv[j].astype(F32)
    gm_ref[...] = gm.astype(BF16)

    l_wo.wait()
    tot = acc[pl.ds(own_q, 512), :]
    tot = jnp.where(lane == 193, 0.0, tot)
    for c in c_o:
        c.wait_recv()
    for j in range(3):
        tot = tot + o_recv[j].astype(F32)
    den = tot[:, 192:193] + tot[:, 193:194]
    attended = (tot[:, 0:192] / den).astype(BF16)

    c_r = []
    for j in (1, 2, 3, 0):
        p = (h + j) % 4
        col = pl.ds(pl.multiple_of(p * 384, 384), 384)
        part = nn_dot(attended[0:256], wo[0:192, col]) + nn_dot(attended[256:512], wo[192:384, col])
        if j:
            r_send[j - 1] = part.astype(BF16)
            c_r.append(send(r_send.at[j - 1], r_recv.at[j - 1], peers[j - 1]))
        else:
            r_own[...] = part
    total = r_own[...]
    for c in c_r:
        c.wait_recv()
    for j in range(3):
        total = total + r_recv[j].astype(F32)
    mixed = (xbuf[h].astype(F32) + total).astype(BF16)
    mbuf[h] = mixed
    c_m = [send(mbuf.at[h], mbuf.at[h], p) for p in peers]
    halo[0, h] = mixed[240:256]
    halo[1, h] = mixed[0:16]
    c_h = []
    for j in range(4):
        c_h.append(send(halo.at[0, h], halo.at[2, h], (nxt, (h + j) % 4)))
        c_h.append(send(halo.at[1, h], halo.at[3, h], (prv, (h + j) % 4)))

    def conv(t, get):
        return sum(nn_dot(get(c), up[t, c * 384 : (c + 1) * 384, :]) for c in range(4))

    for c in c_m:
        c.wait_recv()
    taps = [conv(t, lambda c: mbuf[c]) for t in range(5)]
    for c in c_h:
        c.wait_recv()
    has_prev = (s > 0).astype(F32)
    has_next = (s < 63).astype(F32)
    lo = [conv(t, lambda c: halo[2, c]) * has_prev for t in (0, 1)]
    hi = [conv(t, lambda c: halo[3, c]) * has_next for t in (3, 4)]

    def shifted(v, before, after, which):
        tbuf[which, 0:16, :] = before
        tbuf[which, 16:272, :] = v
        tbuf[which, 272:288, :] = after

    none = jnp.zeros((16, 384), F32)
    shifted(taps[0] + taps[1], lo[0] + lo[1], none, 0)
    shifted(taps[4], none, hi[1], 1)
    shifted(taps[0], lo[0], none, 2)
    shifted(taps[3] + taps[4], none, hi[0] + hi[1], 3)
    even = tbuf[0, 15:271, :] + (taps[2] + taps[3]) + tbuf[1, 17:273, :]
    odd = tbuf[2, 15:271, :] + (taps[1] + taps[2]) + tbuf[3, 17:273, :]
    for c in range(3):
        lanes = slice(c * 128, (c + 1) * 128)
        o32[c, pl.ds(0, 256, stride=2), :] = even[:, lanes]
        o32[c, pl.ds(1, 256, stride=2), :] = odd[:, lanes]
        out_ref[:, lanes] = (o32[c] + lv32[c]).astype(BF16)

    for c in sent + bp + bm + ar + al + [a2r, a2l] + c_gm:
        c.wait_send()


def per_device(level_input, norm_gain, query_weight, key_weight, value_weight, out_weight, up_weight, grad_output):
    any_spec = pl.BlockSpec(memory_space=pl.ANY)
    vmem = pl.BlockSpec(memory_space=pltpu.VMEM)
    v = pltpu.VMEM
    return pl.pallas_call(
        kernel,
        out_shape=(
            jax.ShapeDtypeStruct((512, 384), BF16),
            jax.ShapeDtypeStruct((256, 384), BF16),
        ),
        in_specs=[any_spec] * 8,
        out_specs=(vmem, vmem),
        scratch_shapes=[
            v((512, 384), BF16), v((1, 1536), F32), v((1536, 256), BF16), v((1536, 128), BF16),
            v((1536, 192), BF16), v((384, 1536), BF16), v((5, 1536, 384), BF16), v((544, 384), BF16),
            v((3, 512, 128), F32), v((3, 544, 128), F32), v((4, 256, 384), BF16), v((256, 1536), BF16),
            v((2048, 128), BF16), v((2048, 384), BF16), v((2048, 384), BF16), v((2048, 256), F32),
            v((256, 384), F32), v((3, 256, 384), BF16), v((3, 256, 384), BF16),
            v((3, 512, 256), BF16), v((3, 512, 256), BF16),
            v((256, 384), F32), v((3, 256, 384), BF16), v((3, 256, 384), BF16),
            v((4, 256, 384), BF16), v((4, 4, 16, 384), BF16), v((4, 288, 384), F32), v((3, 512, 128), F32),
            pltpu.SemaphoreType.DMA((8,)),
            pltpu.SemaphoreType.DMA((N_SEM,)),
            pltpu.SemaphoreType.DMA((N_SEM,)),
        ],
        compiler_params=pltpu.CompilerParams(
            collective_id=0, has_side_effects=True, vmem_limit_bytes=56 << 20
        ),
    )(
        level_input, norm_gain.reshape(1, -1), query_weight, key_weight, value_weight,
        out_weight, up_weight, grad_output,
    )


def solution(mesh):
    in_specs = (
        P("seq", "head"), P(), P(None, "head"), P(), P(), P("head", None),
        P(None, None, "head"), P("seq", "head"),
    )
    out_specs = (P("seq", "head"), P("seq", "head"))
    return jax.shard_map(
        per_device, mesh=mesh, in_specs=in_specs, out_specs=out_specs, check_vma=False
    )
```

```python
import functools

import jax
import jax.numpy as jnp
from jax import lax
from jax.experimental import pallas as pl
from jax.experimental.pallas import tpu as pltpu
from jax.sharding import PartitionSpec as P

MESH = pl.DeviceIdType.MESH
F32, BF16 = jnp.float32, jnp.bfloat16
EPS = 1e-06
QSCALE = 24.0 / 128.0 * 1.4426950408889634
N_SEM = 128
RA, RB = 48, 16


def nt_dot(a, b):
    return lax.dot_general(a, b, (((1,), (1,)), ((), ())), preferred_element_type=F32)


def nn_dot(a, b):
    return jnp.dot(a, b, preferred_element_type=F32)


def rms(v):
    return v * lax.rsqrt(jnp.mean(v * v, axis=-1, keepdims=True) + EPS)


def fill(wide, narrow):
    for c in range(3):
        wide[c] = narrow[:, c * 128 : (c + 1) * 128].astype(F32)


def strided(wide, start):
    return jnp.concatenate([wide[c, pl.ds(start, 256, stride=2), :] for c in range(3)], axis=1)


def kernel(
    level_hbm, gain_hbm, wq_hbm, wk_hbm, wv_hbm, wo_hbm, up_hbm, grad_hbm,
    out_ref, gm_ref,
    lv, gain, wq, wk, wv, wo, up, gbuf,
    lv32, g32, xbuf, xq, normed, qall, kva, kvb, acc,
    gm_own, gm_send, gm_recv, o_send, o_recv, mbuf, halo, tbuf, o32,
    load_sem, send_sem, recv_sem,
):
    s = lax.axis_index("seq")
    h = lax.axis_index("head")
    xl, z, y = s // 32, (s // 4) % 8, s % 4
    hs = h + 1 - 2 * (h % 2)
    hx = (h + 2) % 4
    hd = (hs + 2) % 4

    def at(xl_, z_, y_):
        return ((xl_ * 8 + z_) * 4 + y_, h)

    X = at(1 - xl, z, y)
    ZP, ZM = at(xl, (z + 1) % 8, y), at(xl, (z + 7) % 8, y)
    YP, YM = at(xl, z, (y + 1) % 4), at(xl, z, (y + 3) % 4)
    SIB, XH, DIAG = (s, hs), (s, hx), (s, hd)
    XLH = (X[0], hx)
    NXT, PRV = ((s + 1) % 64, h), ((s + 63) % 64, h)

    loads = []

    def load(src, dst):
        c = pltpu.make_async_copy(src, dst, load_sem.at[len(loads)])
        c.start()
        loads.append(c)
        return c

    l_lv = load(level_hbm, lv)
    l_g = load(grad_hbm, gbuf.at[pl.ds(16, 512)])
    l_gain = load(gain_hbm, gain)
    l_wk = load(wk_hbm, wk)
    l_wv = load(wv_hbm, wv)
    l_wq = load(wq_hbm, wq)
    l_up = load(up_hbm, up)
    l_wo = load(wo_hbm, wo.at[h])

    bar = pltpu.get_barrier_semaphore()
    friends = [X, ZP, ZM, YP, YM, SIB, XH, DIAG, XLH, NXT, PRV]
    for f in friends:
        pl.semaphore_signal(bar, inc=1, device_id=f, device_id_type=MESH)

    count = [0]
    sent = []

    def remote(src, dst, dev):
        i = count[0]
        count[0] += 1
        c = pltpu.make_async_remote_copy(
            src_ref=src, dst_ref=dst, send_sem=send_sem.at[i], recv_sem=recv_sem.at[i],
            device_id=dev, device_id_type=MESH,
        )
        sent.append(c)
        return c

    def send(src, dst, dev):
        c = remote(src, dst, dev)
        c.start()
        return c

    def push(ref, dev):
        return send(ref, ref, dev)

    l_lv.wait()
    fill(lv32, lv)
    pooled = 0.5 * (strided(lv32, 0) + strided(lv32, 1))
    xbuf[h] = pooled.astype(BF16)
    l_g.wait()
    own64 = pl.ds(pl.multiple_of(h * 64, 64), 64)
    xq[h] = xbuf[h, own64, :]
    pl.semaphore_wait(bar, len(friends))

    def quarter(p, dev):
        return send(xbuf.at[h, pl.ds(pl.multiple_of(p * 64, 64), 64)], xq.at[h], dev)

    c_quarter = [quarter(hx, XH), quarter(hd, DIAG), quarter(hs, SIB)]
    c_g = [
        send(gbuf.at[pl.ds(512, 16)], gbuf.at[pl.ds(0, 16)], NXT),
        send(gbuf.at[pl.ds(16, 16)], gbuf.at[pl.ds(528, 16)], PRV),
    ]
    x_x = push(xbuf.at[h], XH)
    x_s = push(xbuf.at[h], SIB)

    def normalize(blocks, store):
        sq = sum(jnp.sum(v * v, axis=-1, keepdims=True) for v in blocks)
        inv = lax.rsqrt(sq / 1536.0 + EPS)
        for c in range(4):
            sl = slice(c * 384, (c + 1) * 384)
            store(sl, (blocks[c] * inv * gain[sl].reshape(1, 384)).astype(BF16))

    l_gain.wait()
    l_wk.wait()
    l_wv.wait()
    for c in c_quarter:
        c.wait_recv()
    mine = []
    normalize([xq[c].astype(F32) for c in range(4)], lambda sl, v: mine.append(v))
    mine = jnp.concatenate(mine, axis=1)
    kk = rms(nn_dot(mine, wk[...])).astype(BF16)
    vv = nt_dot(mine, wv[...]).astype(BF16)
    one = (lax.broadcasted_iota(jnp.int32, (64, 64), 1) == 0).astype(BF16)
    kv = jnp.concatenate([kk, vv, one], axis=1)

    def pa(z_, y_, n=1):
        start = (((y_ + 4) % 4) * 8 + (z_ + 8) % 8) * 2 * RA
        return kva.at[pl.ds(pl.multiple_of(start, 2 * RA), 2 * RA)]

    def pb(z_, y_):
        start = (((z_ + 8) % 8) * 4 + (y_ + 4) % 4) * 2 * RB
        return kvb.at[pl.ds(pl.multiple_of(start, 2 * RB), 2 * RB)]

    def gb(z_):
        return kvb.at[pl.ds(pl.multiple_of(((z_ + 8) % 8) * 8 * RB, 8 * RB), 8 * RB)]

    own_a = pl.ds(pl.multiple_of(((y * 8 + z) * 2 + xl) * RA, RA), RA)
    own_b = pl.ds(pl.multiple_of(((z * 4 + y) * 2 + xl) * RB, RB), RB)
    kva[own_a, :] = kv[0:RA]
    kvb[own_b, :] = kv[RA:64]
    c_xa = push(kva.at[own_a], X)
    c_xb = push(kvb.at[own_b], X)

    for c in c_g:
        c.wait_recv()
    fill(g32, gbuf)

    @pl.when(s == 0)
    def _():
        g32[:, 0:16, :] = jnp.zeros((3, 16, 128), F32)

    @pl.when(s == 63)
    def _():
        g32[:, 528:544, :] = jnp.zeros((3, 16, 128), F32)

    rows = [strided(g32, 16 + d) for d in range(-2, 4)]
    pair = [(rows[4 - t] + rows[5 - t]).astype(BF16) for t in range(5)]

    c_xa.wait_recv()
    zr, zl = [push(pa(z, y), ZP)], [push(pa(z, y), ZM)]
    yr, yl = {0: push(pa(z, y), YP)}, {0: push(pa(z, y), YM)}
    c_xb.wait_recv()
    by = [push(pb(z, y), YP), push(pb(z, y), YM)]
    x_x.wait_recv()
    x_f = push(xbuf.at[hx], SIB)
    wo_rows = [slice(0, 128), slice(128, 256), slice(256, 384)]
    l_wo.wait()
    wo_x = [push(wo.at[h, r], XLH) for r in wo_rows]
    wo_s = [push(wo.at[h, r], SIB) for r in wo_rows]

    def grad_block(p):
        return sum(nt_dot(pair[t], up[t, pl.ds(p * 384, 384), :]) for t in range(5))

    def step(k):
        zr[-1].wait_recv()
        if k < 4:
            zr.append(push(pa(z - k, y), ZP))
        yr[-k] = push(pa(z - k, y), YP)
        yl[-k] = push(pa(z - k, y), YM)
        if k < 4:
            zl[-1].wait_recv()
            if k < 3:
                zl.append(push(pa(z + k, y), ZM))
            yr[k] = push(pa(z + k, y), YP)
            yl[k] = push(pa(z + k, y), YM)

    yr2, yl2 = [], []

    def turn(d):
        if d in (0, -1, -2, -3):
            yr[d].wait_recv()
            yr2.append(push(pa(z + d, y - 1), YP))
        else:
            yl[d].wait_recv()
            yl2.append(push(pa(z + d, y + 1), YM))

    l_up.wait()
    gm_send[0] = grad_block(hd).astype(BF16)
    gm_send[1] = grad_block(hs).astype(BF16)
    step(1)
    by[0].wait_recv()
    by2 = push(pb(z, y - 1), YP)
    turn(0)

    x_s.wait_recv()
    x_f.wait_recv()

    def put(sl, v):
        normed[:, sl] = v

    normalize([xbuf[c].astype(F32) for c in range(4)], put)
    l_wq.wait()
    q = nn_dot(normed[...], wq[...])
    for i in range(2):
        qn = (rms(q[:, i * 128 : (i + 1) * 128]) * QSCALE).astype(BF16)
        for p in range(4):
            qall[p, 2 * h + i] = qn[p * 64 : (p + 1) * 64]

    def heads(c):
        return qall.at[:, pl.ds(2 * c, 2)]

    q_x = push(heads(h), XH)
    q_s = push(heads(h), SIB)
    step(2)
    by[1].wait_recv()
    by2.wait_recv()
    bp = [remote(gb(z - i), gb(z - i), ZP) for i in range(3)]
    bm = [remote(gb(z + i), gb(z + i), ZM) for i in range(4)]
    bp[0].start()
    bm[0].start()
    turn(-1)
    turn(1)
    gm_own[0] = grad_block(hx)
    step(3)
    turn(-2)
    turn(2)
    q_x.wait_recv()
    q_f = push(heads(hx), SIB)
    gm_1 = [send(gm_send.at[i], gm_recv.at[i], SIB) for i in range(2)]
    gm_own[1] = grad_block(h)
    step(4)
    turn(-3)
    turn(3)
    acc[...] = jnp.zeros_like(acc)
    q_s.wait_recv()
    q_f.wait_recv()
    gm_2 = remote(gm_send.at[2], gm_recv.at[2], XH)

    def keys_values(i):
        ya = (y + i + i // 2 - 2 * (i // 3)) % 4
        oa = pl.multiple_of(ya * 16 * RA, 16 * RA)
        ob0 = pl.multiple_of(((z - i + 8) % 8) * 8 * RB, 8 * RB)
        ob1 = pl.multiple_of(((z + i + 1) % 8) * 8 * RB, 8 * RB)
        ka = jnp.concatenate(
            [kva[pl.ds(oa, 16 * RA), :], kvb[pl.ds(ob0, 8 * RB), :], kvb[pl.ds(ob1, 8 * RB), :]],
            axis=0,
        )
        return ka[:, 0:128], ka[:, 128:384]

    def attend(p, keys, vals):
        w = jnp.exp2(nt_dot(qall[p].reshape(512, 128), keys)).astype(BF16)
        return nn_dot(w, vals)

    yr2_3 = pa(z - 4, y + 1)
    last_l = remote(yr2_3, yr2_3, YM)

    @pl.loop(0, 3)
    def _(i):
        @pl.when(i == 0)
        def _():
            bm[0].wait_recv()
            bm[1].start()
            bp[0].wait_recv()
            bp[1].start()

        @pl.when(i == 1)
        def _():
            yl[-4].wait_recv()
            last_l.start()
            for d in (0, -1, -2, -3):
                yl[d].wait_recv()
            bm[1].wait_recv()
            bm[2].start()
            gm_1[0].wait_recv()
            gm_send[2] = (gm_own[0] + gm_recv[0].astype(F32)).astype(BF16)
            gm_2.start()

        @pl.when(i == 2)
        def _():
            for d in (1, 2, 3, -4):
                yr[d].wait_recv()
            bp[1].wait_recv()
            bp[2].start()
            bm[2].wait_recv()
            bm[3].start()

        keys, vals = keys_values(i)
        for p in range(4):
            acc[p] += attend(p, keys, vals)

    for c in yr2 + yl2 + [last_l, bp[2], bm[3]]:
        c.wait_recv()
    keys, vals = keys_values(3)
    lane = lax.broadcasted_iota(jnp.int32, (512, 256), 1)

    def packed(part):
        den = part[:, 192:193]
        low = den - den.astype(BF16).astype(F32)
        return jnp.where(lane == 193, low, part).astype(BF16)

    o_1 = []
    for i, p in enumerate((hd, hs)):
        o_send[i] = packed(acc[p] + attend(p, keys, vals))
        o_1.append(send(o_send.at[i], o_recv.at[i], SIB))
    for p in (hx, h):
        acc[p] += attend(p, keys, vals)

    def clear(part):
        return jnp.where(lane == 193, 0.0, part)

    def widen(part):
        part = part.astype(F32)
        return jnp.where(lane == 192, part + part[:, 193:194], clear(part))

    o_1[0].wait_recv()
    o_send[2] = packed(clear(acc[hx]) + widen(o_recv[0]))
    o_2 = send(o_send.at[2], o_recv.at[2], XH)

    wo_f = []
    for i, r in enumerate(wo_rows):
        wo_x[i].wait_recv()
        wo_f.append(push(wo.at[hx, r], SIB))

    o_1[1].wait_recv()
    tot = clear(acc[h]) + widen(o_recv[1])
    gm_1[1].wait_recv()
    gm_2.wait_recv()
    gm_ref[...] = (gm_own[1] + gm_recv[1].astype(F32) + gm_recv[2].astype(F32)).astype(BF16)
    for c in wo_s + wo_f:
        c.wait_recv()
    o_2.wait_recv()
    tot = tot + widen(o_recv[2])
    att = (tot[:, 0:192] / tot[:, 192:193]).astype(BF16)
    att = jnp.concatenate([att[g * 64 : (g + 1) * 64] for g in range(8)], axis=1)
    mixed = jnp.concatenate([xq[c] for c in range(4)], axis=1).astype(F32)
    for c in range(4):
        mixed = mixed + nn_dot(att[:, c * 384 : (c + 1) * 384], wo[c])
    mbuf[h] = mixed.astype(BF16)
    m_x = push(mbuf.at[h], XH)
    m_s = push(mbuf.at[h], SIB)
    m_x.wait_recv()
    m_f = push(mbuf.at[hx], SIB)
    m_s.wait_recv()
    m_f.wait_recv()
    c_h = [
        send(mbuf.at[3, pl.ds(48, 16)], halo.at[0], NXT),
        send(mbuf.at[0, pl.ds(0, 16)], halo.at[1], PRV),
    ]

    full = mbuf[...].reshape(256, 1536)
    taps = [nn_dot(full, up[t]) for t in range(5)]
    for c in c_h:
        c.wait_recv()
    has_prev = (s > 0).astype(F32)
    has_next = (s < 63).astype(F32)
    lo = [nn_dot(halo[0], up[t]) * has_prev for t in (0, 1)]
    hi = [nn_dot(halo[1], up[t]) * has_next for t in (3, 4)]

    def shifted(v, before, after, which):
        tbuf[which, 0:16, :] = before
        tbuf[which, 16:272, :] = v
        tbuf[which, 272:288, :] = after

    none = jnp.zeros((16, 384), F32)
    shifted(taps[0] + taps[1], lo[0] + lo[1], none, 0)
    shifted(taps[4], none, hi[1], 1)
    shifted(taps[0], lo[0], none, 2)
    shifted(taps[3] + taps[4], none, hi[0] + hi[1], 3)
    even = tbuf[0, 15:271, :] + (taps[2] + taps[3]) + tbuf[1, 17:273, :]
    odd = tbuf[2, 15:271, :] + (taps[1] + taps[2]) + tbuf[3, 17:273, :]
    for c in range(3):
        lanes = slice(c * 128, (c + 1) * 128)
        o32[c, pl.ds(0, 256, stride=2), :] = even[:, lanes]
        o32[c, pl.ds(1, 256, stride=2), :] = odd[:, lanes]
        out_ref[:, lanes] = (o32[c] + lv32[c]).astype(BF16)

    for c in sent:
        c.wait_send()


def per_device(level_input, norm_gain, query_weight, key_weight, value_weight, out_weight, up_weight, grad_output):
    any_spec = pl.BlockSpec(memory_space=pl.ANY)
    vmem = pl.BlockSpec(memory_space=pltpu.VMEM)
    v = pltpu.VMEM
    outs = pl.pallas_call(
        kernel,
        out_shape=(
            jax.ShapeDtypeStruct((512, 384), BF16),
            jax.ShapeDtypeStruct((256, 384), BF16),
        ),
        in_specs=[any_spec] * 8,
        out_specs=(vmem, vmem),
        scratch_shapes=[
            v((512, 384), BF16), v((1536,), F32), v((1536, 256), BF16), v((1536, 128), BF16),
            v((192, 1536), BF16), v((4, 384, 1536), BF16), v((5, 1536, 384), BF16), v((544, 384), BF16),
            v((3, 512, 128), F32), v((3, 544, 128), F32), v((4, 256, 384), BF16), v((4, 64, 384), BF16),
            v((256, 1536), BF16), v((4, 8, 64, 128), BF16), v((64 * RA, 384), BF16),
            v((64 * RB, 384), BF16), v((4, 512, 256), F32),
            v((2, 256, 384), F32), v((3, 256, 384), BF16), v((3, 256, 384), BF16),
            v((3, 512, 256), BF16), v((3, 512, 256), BF16),
            v((4, 64, 1536), BF16), v((2, 16, 1536), BF16), v((4, 288, 384), F32), v((3, 512, 128), F32),
            pltpu.SemaphoreType.DMA((8,)),
            pltpu.SemaphoreType.DMA((N_SEM,)),
            pltpu.SemaphoreType.DMA((N_SEM,)),
        ],
        compiler_params=pltpu.CompilerParams(
            collective_id=0, has_side_effects=True, vmem_limit_bytes=56 << 20
        ),
    )(
        level_input, norm_gain, query_weight, key_weight, value_weight.T,
        out_weight, up_weight, grad_output,
    )
    return outs


def solution(mesh):
    in_specs = (
        P("seq", "head"), P(), P(None, "head"), P(), P(), P("head", None),
        P(None, None, "head"), P("seq", "head"),
    )
    out_specs = (P("seq", "head"), P("seq", "head"))
    return jax.shard_map(
        per_device, mesh=mesh, in_specs=in_specs, out_specs=out_specs, check_vma=False
    )
```

```python
import functools

import jax
import jax.numpy as jnp
from jax import lax
from jax.experimental import pallas as pl
from jax.experimental.pallas import tpu as pltpu
from jax.sharding import PartitionSpec as P

MESH = pl.DeviceIdType.MESH
F32, BF16 = jnp.float32, jnp.bfloat16
EPS = 1e-06
QSCALE = 24.0 / 128.0 * 1.4426950408889634
N_SEM = 128
RA, RB = 48, 16


def nt_dot(a, b):
    return lax.dot_general(a, b, (((1,), (1,)), ((), ())), preferred_element_type=F32)


def nn_dot(a, b):
    return jnp.dot(a, b, preferred_element_type=F32)


def rms(v):
    return v * lax.rsqrt(jnp.mean(v * v, axis=-1, keepdims=True) + EPS)


def fill(wide, narrow):
    for c in range(3):
        wide[c] = narrow[:, c * 128 : (c + 1) * 128].astype(F32)


def strided(wide, start):
    return jnp.concatenate([wide[c, pl.ds(start, 256, stride=2), :] for c in range(3)], axis=1)


def kernel(
    level_hbm, gain_hbm, wq_hbm, wk_hbm, wv_hbm, wo_hbm, up_hbm, grad_hbm,
    out_ref, gm_ref,
    lv, gain, wq, wk, wv, wo, up, gbuf,
    lv32, g32, xbuf, xq, normed, qall, kvx, kva, kvb, acc,
    gm_own, gm_send, gm_recv, o_send, o_recv, mbuf, halo, tbuf, o32,
    load_sem, send_sem, recv_sem,
):
    s = lax.axis_index("seq")
    h = lax.axis_index("head")
    xl, z, y = s // 32, (s // 4) % 8, s % 4
    hs = h + 1 - 2 * (h % 2)
    hx = (h + 2) % 4
    hd = (hs + 2) % 4

    def at(xl_, z_, y_):
        return ((xl_ * 8 + z_) * 4 + y_, h)

    X = at(1 - xl, z, y)
    ZP, ZM = at(xl, (z + 1) % 8, y), at(xl, (z + 7) % 8, y)
    YP, YM = at(xl, z, (y + 1) % 4), at(xl, z, (y + 3) % 4)
    SIB, XH, DIAG = (s, hs), (s, hx), (s, hd)
    XLH = (X[0], hx)
    NXT, PRV = ((s + 1) % 64, h), ((s + 63) % 64, h)

    loads = []

    def load(src, dst):
        c = pltpu.make_async_copy(src, dst, load_sem.at[len(loads)])
        c.start()
        loads.append(c)
        return c

    l_lv = load(level_hbm, lv)
    l_g = load(grad_hbm, gbuf.at[pl.ds(16, 512)])
    l_gain = load(gain_hbm, gain)
    l_wk = load(wk_hbm, wk)
    l_wv = load(wv_hbm, wv)
    l_wq = load(wq_hbm, wq)
    l_up = load(up_hbm, up)
    l_wo = load(wo_hbm, wo.at[h])

    bar = pltpu.get_barrier_semaphore()
    friends = [X, ZP, ZM, YP, YM, SIB, XH, DIAG, XLH, NXT, PRV]
    for f in friends:
        pl.semaphore_signal(bar, inc=1, device_id=f, device_id_type=MESH)

    count = [0]
    sent = []

    def remote(src, dst, dev):
        i = count[0]
        count[0] += 1
        c = pltpu.make_async_remote_copy(
            src_ref=src, dst_ref=dst, send_sem=send_sem.at[i], recv_sem=recv_sem.at[i],
            device_id=dev, device_id_type=MESH,
        )
        sent.append(c)
        return c

    def send(src, dst, dev):
        c = remote(src, dst, dev)
        c.start()
        return c

    def push(ref, dev):
        return send(ref, ref, dev)

    l_lv.wait()
    fill(lv32, lv)
    pooled = 0.5 * (strided(lv32, 0) + strided(lv32, 1))
    xbuf[h] = pooled.astype(BF16)
    l_g.wait()
    own64 = pl.ds(pl.multiple_of(h * 64, 64), 64)
    xq[h] = xbuf[h, own64, :]
    pl.semaphore_wait(bar, len(friends))

    def quarter(p, dev):
        return send(xbuf.at[h, pl.ds(pl.multiple_of(p * 64, 64), 64)], xq.at[h], dev)

    c_quarter = [quarter(hx, XH), quarter(hd, DIAG), quarter(hs, SIB)]
    c_g = [
        send(gbuf.at[pl.ds(512, 16)], gbuf.at[pl.ds(0, 16)], NXT),
        send(gbuf.at[pl.ds(16, 16)], gbuf.at[pl.ds(528, 16)], PRV),
    ]
    x_x = push(xbuf.at[h], XH)
    x_s = push(xbuf.at[h], SIB)

    def normalize(blocks, store):
        sq = sum(jnp.sum(v * v, axis=-1, keepdims=True) for v in blocks)
        inv = lax.rsqrt(sq / 1536.0 + EPS)
        for c in range(4):
            sl = slice(c * 384, (c + 1) * 384)
            store(sl, (blocks[c] * inv * gain[sl].reshape(1, 384)).astype(BF16))

    l_gain.wait()
    l_wk.wait()
    l_wv.wait()
    for c in c_quarter:
        c.wait_recv()
    mine = []
    normalize([xq[c].astype(F32) for c in range(4)], lambda sl, v: mine.append(v))
    mine = jnp.concatenate(mine, axis=1)
    kk = rms(nn_dot(mine, wk[...])).astype(BF16)
    vv = nt_dot(mine, wv[...]).astype(BF16)
    one = (lax.broadcasted_iota(jnp.int32, (64, 64), 1) == 0).astype(BF16)
    kv = jnp.concatenate([kk, vv, one], axis=1)

    def pa(z_, y_):
        return kva.at[((y_ + 4) % 4) * 8 + (z_ + 8) % 8]

    def pb(z_, y_):
        return kvb.at[((z_ + 8) % 8) * 4 + (y_ + 4) % 4]

    def gb(z_):
        return kvb.at[pl.ds(((z_ + 8) % 8) * 4, 4)]

    kvx[xl] = kv
    c_x = push(kvx.at[xl], X)

    for c in c_g:
        c.wait_recv()
    fill(g32, gbuf)

    @pl.when(s == 0)
    def _():
        g32[:, 0:16, :] = jnp.zeros((3, 16, 128), F32)

    @pl.when(s == 63)
    def _():
        g32[:, 528:544, :] = jnp.zeros((3, 16, 128), F32)

    rows = [strided(g32, 16 + d) for d in range(-2, 4)]
    pair = [(rows[4 - t] + rows[5 - t]).astype(BF16) for t in range(5)]

    c_x.wait_recv()

    def pack(dst, slot, first, n):
        left, right = kvx[0, first : first + n, :], kvx[1, first : first + n, :]
        dst[slot, 0:n] = left[:, 0:128]
        dst[slot, n : 2 * n] = right[:, 0:128]
        dst[slot, 2 * n : 3 * n] = left[:, 128:256]
        dst[slot, 3 * n : 4 * n] = right[:, 128:256]
        dst[slot, 4 * n : 5 * n] = jnp.concatenate([left[:, 256:320], right[:, 256:320]], axis=1)

    pack(kva, y * 8 + z, 0, RA)
    pack(kvb, z * 4 + y, RA, RB)
    zr, zl = [push(pa(z, y), ZP)], [push(pa(z, y), ZM)]
    yr, yl = {0: push(pa(z, y), YP)}, {0: push(pa(z, y), YM)}
    by = [push(pb(z, y), YP), push(pb(z, y), YM)]
    x_x.wait_recv()
    x_f = push(xbuf.at[hx], SIB)
    wo_rows = [slice(0, 128), slice(128, 256), slice(256, 384)]
    l_wo.wait()
    wo_x = [push(wo.at[h, r], XLH) for r in wo_rows]
    wo_s = [push(wo.at[h, r], SIB) for r in wo_rows]

    def grad_block(p):
        return sum(nt_dot(pair[t], up[t, pl.ds(p * 384, 384), :]) for t in range(5))

    def step(k):
        zr[-1].wait_recv()
        if k < 4:
            zr.append(push(pa(z - k, y), ZP))
        yr[-k] = push(pa(z - k, y), YP)
        yl[-k] = push(pa(z - k, y), YM)
        if k < 4:
            zl[-1].wait_recv()
            if k < 3:
                zl.append(push(pa(z + k, y), ZM))
            yr[k] = push(pa(z + k, y), YP)
            yl[k] = push(pa(z + k, y), YM)

    yr2, yl2 = [], []

    def turn(d):
        if d in (0, -1, -2, -3):
            yr[d].wait_recv()
            yr2.append(push(pa(z + d, y - 1), YP))
        else:
            yl[d].wait_recv()
            yl2.append(push(pa(z + d, y + 1), YM))

    l_up.wait()
    gm_send[0] = grad_block(hd).astype(BF16)
    gm_send[1] = grad_block(hs).astype(BF16)
    step(1)
    by[0].wait_recv()
    by2 = push(pb(z, y - 1), YP)
    turn(0)

    x_s.wait_recv()
    x_f.wait_recv()

    def put(sl, v):
        normed[:, sl] = v

    normalize([xbuf[c].astype(F32) for c in range(4)], put)
    l_wq.wait()
    q = nn_dot(normed[...], wq[...])
    for i in range(2):
        qn = (rms(q[:, i * 128 : (i + 1) * 128]) * QSCALE).astype(BF16)
        for p in range(4):
            qall[p, 2 * h + i] = qn[p * 64 : (p + 1) * 64]

    def heads(c):
        return qall.at[:, pl.ds(2 * c, 2)]

    q_x = push(heads(h), XH)
    q_s = push(heads(h), SIB)
    step(2)
    by[1].wait_recv()
    by2.wait_recv()
    bp = [remote(gb(z - i), gb(z - i), ZP) for i in range(3)]
    bm = [remote(gb(z + i), gb(z + i), ZM) for i in range(4)]
    bp[0].start()
    bm[0].start()
    turn(-1)
    turn(1)
    gm_own[0] = grad_block(hx)
    step(3)
    turn(-2)
    turn(2)
    q_x.wait_recv()
    q_f = push(heads(hx), SIB)
    gm_1 = [send(gm_send.at[i], gm_recv.at[i], SIB) for i in range(2)]
    gm_own[1] = grad_block(h)
    step(4)
    turn(-3)
    turn(3)
    acc[...] = jnp.zeros_like(acc)
    q_s.wait_recv()
    q_f.wait_recv()
    gm_2 = remote(gm_send.at[2], gm_recv.at[2], XH)

    def keys_values(i):
        ya = (y + i + i // 2 - 2 * (i // 3)) % 4
        keys, vals = [], []
        for group, n in (
            (kva[pl.ds(ya * 8, 8)], RA),
            (kvb[pl.ds(((z - i + 8) % 8) * 4, 4)], RB),
            (kvb[pl.ds(((z + i + 1) % 8) * 4, 4)], RB),
        ):
            slots = group.shape[0]
            rest = group[:, 4 * n : 5 * n]
            turned = jnp.concatenate([rest[:, :, 64:128], rest[:, :, 0:64]], axis=2)
            rest = jnp.concatenate([rest, turned], axis=1).reshape(slots * 2 * n, 128)
            at_lane = lax.broadcasted_iota(jnp.int32, rest.shape, 1)
            rest = jnp.where(at_lane < 64, rest, (at_lane == 64).astype(BF16))
            keys.append(group[:, 0 : 2 * n].reshape(slots * 2 * n, 128))
            first = group[:, 2 * n : 4 * n].reshape(slots * 2 * n, 128)
            vals.append(jnp.concatenate([first, rest], axis=1))
        return jnp.concatenate(keys, axis=0), jnp.concatenate(vals, axis=0)

    def attend(p, keys, vals):
        w = jnp.exp2(nt_dot(qall[p].reshape(512, 128), keys)).astype(BF16)
        return nn_dot(w, vals)

    yr2_3 = pa(z - 4, y + 1)
    last_l = remote(yr2_3, yr2_3, YM)

    wo_f = [remote(wo.at[hx, r], wo.at[hx, r], SIB) for r in wo_rows]

    @pl.loop(0, 3)
    def _(i):
        @pl.when(i == 0)
        def _():
            bm[0].wait_recv()
            bm[1].start()
            bp[0].wait_recv()
            bp[1].start()

        @pl.when(i == 1)
        def _():
            yl[-4].wait_recv()
            last_l.start()
            for d in (0, -1, -2, -3):
                yl[d].wait_recv()
            bm[1].wait_recv()
            bm[2].start()
            gm_1[0].wait_recv()
            gm_send[2] = (gm_own[0] + gm_recv[0].astype(F32)).astype(BF16)
            gm_2.start()
            wo_x[0].wait_recv()
            wo_f[0].start()

        @pl.when(i == 2)
        def _():
            wo_x[1].wait_recv()
            wo_f[1].start()
            for d in (1, 2, 3, -4):
                yr[d].wait_recv()
            bp[1].wait_recv()
            bp[2].start()
            bm[2].wait_recv()
            bm[3].start()

        keys, vals = keys_values(i)
        for p in range(4):
            acc[p] += attend(p, keys, vals)

    for c in yr2 + yl2 + [last_l, bp[2], bm[3]]:
        c.wait_recv()
    keys, vals = keys_values(3)
    lane = lax.broadcasted_iota(jnp.int32, (512, 256), 1)

    def packed(part):
        den = part[:, 192:193]
        low = den - den.astype(BF16).astype(F32)
        return jnp.where(lane == 193, low, part).astype(BF16)

    o_1 = []
    for i, p in enumerate((hd, hs)):
        o_send[i] = packed(acc[p] + attend(p, keys, vals))
        o_1.append(send(o_send.at[i], o_recv.at[i], SIB))
    for p in (hx, h):
        acc[p] += attend(p, keys, vals)

    def clear(part):
        return jnp.where(lane == 193, 0.0, part)

    def widen(part):
        part = part.astype(F32)
        return jnp.where(lane == 192, part + part[:, 193:194], clear(part))

    o_1[0].wait_recv()
    o_send[2] = packed(clear(acc[hx]) + widen(o_recv[0]))
    o_2 = send(o_send.at[2], o_recv.at[2], XH)

    wo_x[2].wait_recv()
    wo_f[2].start()

    o_1[1].wait_recv()
    tot = clear(acc[h]) + widen(o_recv[1])
    gm_1[1].wait_recv()
    gm_2.wait_recv()
    gm_ref[...] = (gm_own[1] + gm_recv[1].astype(F32) + gm_recv[2].astype(F32)).astype(BF16)
    for c in wo_s + wo_f:
        c.wait_recv()
    o_2.wait_recv()
    tot = tot + widen(o_recv[2])
    att = (tot[:, 0:192] / tot[:, 192:193]).astype(BF16)
    att = jnp.concatenate([att[g * 64 : (g + 1) * 64] for g in range(8)], axis=1)
    pooled = jnp.concatenate([xq[c] for c in range(4)], axis=1).astype(F32)
    m_x, m_s, m_f = [], [], []
    for c in range(3):
        col = slice(c * 512, (c + 1) * 512)
        part = pooled[:, col]
        for b in range(4):
            part = part + nn_dot(att[:, b * 384 : (b + 1) * 384], wo[b, :, col])
        mbuf[c, h] = part.astype(BF16)
        m_x.append(push(mbuf.at[c, h], XH))
        m_s.append(push(mbuf.at[c, h], SIB))
    for c in range(3):
        m_x[c].wait_recv()
        m_f.append(push(mbuf.at[c, hx], SIB))
    c_h = []
    taps = [0.0] * 5
    for c in range(3):
        m_s[c].wait_recv()
        m_f[c].wait_recv()
        c_h.append(send(mbuf.at[c, 3, pl.ds(48, 16)], halo.at[0, c], NXT))
        c_h.append(send(mbuf.at[c, 0, pl.ds(0, 16)], halo.at[1, c], PRV))
        full = mbuf[c].reshape(256, 512)
        for t in range(5):
            taps[t] = taps[t] + nn_dot(full, up[t, c * 512 : (c + 1) * 512, :])

    def edge(side, t):
        return sum(nn_dot(halo[side, c], up[t, c * 512 : (c + 1) * 512, :]) for c in range(3))

    for c in c_h:
        c.wait_recv()
    has_prev = (s > 0).astype(F32)
    has_next = (s < 63).astype(F32)
    lo = [edge(0, t) * has_prev for t in (0, 1)]
    hi = [edge(1, t) * has_next for t in (3, 4)]

    def shifted(v, before, after, which):
        tbuf[which, 0:16, :] = before
        tbuf[which, 16:272, :] = v
        tbuf[which, 272:288, :] = after

    none = jnp.zeros((16, 384), F32)
    shifted(taps[0] + taps[1], lo[0] + lo[1], none, 0)
    shifted(taps[4], none, hi[1], 1)
    shifted(taps[0], lo[0], none, 2)
    shifted(taps[3] + taps[4], none, hi[0] + hi[1], 3)
    even = tbuf[0, 15:271, :] + (taps[2] + taps[3]) + tbuf[1, 17:273, :]
    odd = tbuf[2, 15:271, :] + (taps[1] + taps[2]) + tbuf[3, 17:273, :]
    for c in range(3):
        lanes = slice(c * 128, (c + 1) * 128)
        o32[c, pl.ds(0, 256, stride=2), :] = even[:, lanes]
        o32[c, pl.ds(1, 256, stride=2), :] = odd[:, lanes]
        out_ref[:, lanes] = (o32[c] + lv32[c]).astype(BF16)

    for c in sent:
        c.wait_send()


def per_device(level_input, norm_gain, query_weight, key_weight, value_weight, out_weight, up_weight, grad_output):
    any_spec = pl.BlockSpec(memory_space=pl.ANY)
    vmem = pl.BlockSpec(memory_space=pltpu.VMEM)
    v = pltpu.VMEM
    outs = pl.pallas_call(
        kernel,
        out_shape=(
            jax.ShapeDtypeStruct((512, 384), BF16),
            jax.ShapeDtypeStruct((256, 384), BF16),
        ),
        in_specs=[any_spec] * 8,
        out_specs=(vmem, vmem),
        scratch_shapes=[
            v((512, 384), BF16), v((1536,), F32), v((1536, 256), BF16), v((1536, 128), BF16),
            v((192, 1536), BF16), v((4, 384, 1536), BF16), v((5, 1536, 384), BF16), v((544, 384), BF16),
            v((3, 512, 128), F32), v((3, 544, 128), F32), v((4, 256, 384), BF16), v((4, 64, 384), BF16),
            v((256, 1536), BF16), v((4, 8, 64, 128), BF16), v((2, 64, 384), BF16), v((32, 5 * RA, 128), BF16),
            v((32, 5 * RB, 128), BF16), v((4, 512, 256), F32),
            v((2, 256, 384), F32), v((3, 256, 384), BF16), v((3, 256, 384), BF16),
            v((3, 512, 256), BF16), v((3, 512, 256), BF16),
            v((3, 4, 64, 512), BF16), v((2, 3, 16, 512), BF16), v((4, 288, 384), F32), v((3, 512, 128), F32),
            pltpu.SemaphoreType.DMA((8,)),
            pltpu.SemaphoreType.DMA((N_SEM,)),
            pltpu.SemaphoreType.DMA((N_SEM,)),
        ],
        compiler_params=pltpu.CompilerParams(
            collective_id=0, has_side_effects=True, vmem_limit_bytes=56 << 20
        ),
    )(
        level_input, norm_gain, query_weight, key_weight, value_weight.T,
        out_weight, up_weight, grad_output,
    )
    return outs


def solution(mesh):
    in_specs = (
        P("seq", "head"), P(), P(None, "head"), P(), P(), P("head", None),
        P(None, None, "head"), P("seq", "head"),
    )
    out_specs = (P("seq", "head"), P("seq", "head"))
    return jax.shard_map(
        per_device, mesh=mesh, in_specs=in_specs, out_specs=out_specs, check_vma=False
    )
```

```python
import functools

import jax
import jax.numpy as jnp
from jax import lax
from jax.experimental import pallas as pl
from jax.experimental.pallas import tpu as pltpu
from jax.sharding import PartitionSpec as P

MESH = pl.DeviceIdType.MESH
F32, BF16 = jnp.float32, jnp.bfloat16
EPS = 1e-06
QSCALE = 24.0 / 128.0 * 1.4426950408889634
N_SEM = 128
RA, RB = 48, 16


def nt_dot(a, b):
    return lax.dot_general(a, b, (((1,), (1,)), ((), ())), preferred_element_type=F32)


def nn_dot(a, b):
    return jnp.dot(a, b, preferred_element_type=F32)


def rms(v):
    return v * lax.rsqrt(jnp.mean(v * v, axis=-1, keepdims=True) + EPS)


def fill(wide, narrow):
    for c in range(3):
        wide[c] = narrow[:, c * 128 : (c + 1) * 128].astype(F32)


def strided(wide, start):
    return jnp.concatenate([wide[c, pl.ds(start, 256, stride=2), :] for c in range(3)], axis=1)


def kernel(
    level_hbm, gain_hbm, wq_hbm, wk_hbm, wv_hbm, wo_hbm, up_hbm, grad_hbm,
    out_ref, gm_ref,
    lv, gain, wq, wk, wv, wo, up, gbuf,
    lv32, g32, xbuf, xq, normed, qall, kvx, kva, kvb, acc,
    gm_own, gm_send, gm_recv, o_send, o_recv, mbuf, halo, tbuf, o32,
    load_sem, send_sem, recv_sem,
):
    s = lax.axis_index("seq")
    h = lax.axis_index("head")
    xl, z, y = s // 32, (s // 4) % 8, s % 4
    hs = h + 1 - 2 * (h % 2)
    hx = (h + 2) % 4
    hd = (hs + 2) % 4

    def at(xl_, z_, y_):
        return ((xl_ * 8 + z_) * 4 + y_, h)

    X = at(1 - xl, z, y)
    ZP, ZM = at(xl, (z + 1) % 8, y), at(xl, (z + 7) % 8, y)
    YP, YM = at(xl, z, (y + 1) % 4), at(xl, z, (y + 3) % 4)
    SIB, XH, DIAG = (s, hs), (s, hx), (s, hd)
    XLH = (X[0], hx)
    NXT, PRV = ((s + 1) % 64, h), ((s + 63) % 64, h)

    loads = []

    def load(src, dst):
        c = pltpu.make_async_copy(src, dst, load_sem.at[len(loads)])
        c.start()
        loads.append(c)
        return c

    l_lv = load(level_hbm, lv)
    l_g = load(grad_hbm, gbuf.at[pl.ds(16, 512)])
    l_gain = load(gain_hbm, gain)
    l_wk = load(wk_hbm, wk)
    l_wv = load(wv_hbm, wv)
    l_wq = load(wq_hbm, wq)
    l_up = load(up_hbm, up)
    l_wo = load(wo_hbm, wo.at[h])

    bar = pltpu.get_barrier_semaphore()
    friends = [X, ZP, ZM, YP, YM, SIB, XH, DIAG, XLH, NXT, PRV]
    for f in friends:
        pl.semaphore_signal(bar, inc=1, device_id=f, device_id_type=MESH)

    count = [0]
    sent = []

    def remote(src, dst, dev):
        i = count[0]
        count[0] += 1
        c = pltpu.make_async_remote_copy(
            src_ref=src, dst_ref=dst, send_sem=send_sem.at[i], recv_sem=recv_sem.at[i],
            device_id=dev, device_id_type=MESH,
        )
        sent.append(c)
        return c

    def send(src, dst, dev):
        c = remote(src, dst, dev)
        c.start()
        return c

    def push(ref, dev):
        return send(ref, ref, dev)

    l_lv.wait()
    fill(lv32, lv)
    pooled = 0.5 * (strided(lv32, 0) + strided(lv32, 1))
    xbuf[h] = pooled.astype(BF16)
    l_g.wait()
    own64 = pl.ds(pl.multiple_of(h * 64, 64), 64)
    xq[h] = xbuf[h, own64, :]
    pl.semaphore_wait(bar, len(friends))

    def quarter(p, dev):
        return send(xbuf.at[h, pl.ds(pl.multiple_of(p * 64, 64), 64)], xq.at[h], dev)

    c_quarter = [quarter(hx, XH), quarter(hd, DIAG), quarter(hs, SIB)]
    c_g = [
        send(gbuf.at[pl.ds(512, 16)], gbuf.at[pl.ds(0, 16)], NXT),
        send(gbuf.at[pl.ds(16, 16)], gbuf.at[pl.ds(528, 16)], PRV),
    ]
    x_x = push(xbuf.at[h], XH)
    x_s = push(xbuf.at[h], SIB)

    def normalize(blocks, store):
        sq = sum(jnp.sum(v * v, axis=-1, keepdims=True) for v in blocks)
        inv = lax.rsqrt(sq / 1536.0 + EPS)
        for c in range(4):
            sl = slice(c * 384, (c + 1) * 384)
            store(sl, (blocks[c] * inv * gain[sl].reshape(1, 384)).astype(BF16))

    l_gain.wait()
    l_wk.wait()
    l_wv.wait()
    for c in c_quarter:
        c.wait_recv()
    mine = []
    normalize([xq[c].astype(F32) for c in range(4)], lambda sl, v: mine.append(v))
    mine = jnp.concatenate(mine, axis=1)
    kk = rms(nn_dot(mine, wk[...])).astype(BF16)
    vv = nt_dot(mine, wv[...]).astype(BF16)
    one = (lax.broadcasted_iota(jnp.int32, (64, 64), 1) == 0).astype(BF16)
    kv = jnp.concatenate([kk, vv, one], axis=1)

    def pa(z_, y_):
        return kva.at[((y_ + 4) % 4) * 8 + (z_ + 8) % 8]

    def pb(z_, y_):
        return kvb.at[((z_ + 8) % 8) * 4 + (y_ + 4) % 4]

    def gb(z_):
        return kvb.at[pl.ds(((z_ + 8) % 8) * 4, 4)]

    kvx[xl] = kv
    c_x = push(kvx.at[xl], X)

    for c in c_g:
        c.wait_recv()
    fill(g32, gbuf)

    @pl.when(s == 0)
    def _():
        g32[:, 0:16, :] = jnp.zeros((3, 16, 128), F32)

    @pl.when(s == 63)
    def _():
        g32[:, 528:544, :] = jnp.zeros((3, 16, 128), F32)

    rows = [strided(g32, 16 + d) for d in range(-2, 4)]
    pair = [(rows[4 - t] + rows[5 - t]).astype(BF16) for t in range(5)]

    c_x.wait_recv()

    def pack(dst, slot, first, n):
        left, right = kvx[0, first : first + n, :], kvx[1, first : first + n, :]
        dst[slot, 0:n] = left[:, 0:128]
        dst[slot, n : 2 * n] = right[:, 0:128]
        dst[slot, 2 * n : 3 * n] = left[:, 128:256]
        dst[slot, 3 * n : 4 * n] = right[:, 128:256]
        dst[slot, 4 * n : 5 * n] = jnp.concatenate([left[:, 256:320], right[:, 256:320]], axis=1)

    pack(kva, y * 8 + z, 0, RA)
    pack(kvb, z * 4 + y, RA, RB)
    zr, zl = [push(pa(z, y), ZP)], [push(pa(z, y), ZM)]
    yr, yl = {0: push(pa(z, y), YP)}, {0: push(pa(z, y), YM)}
    by = [push(pb(z, y), YP), push(pb(z, y), YM)]
    x_x.wait_recv()
    x_f = push(xbuf.at[hx], SIB)
    wo_rows = [slice(0, 128), slice(128, 256), slice(256, 384)]
    l_wo.wait()
    wo_x = [push(wo.at[h, r], XLH) for r in wo_rows]
    wo_s = [push(wo.at[h, r], SIB) for r in wo_rows]

    def grad_block(p):
        return sum(nt_dot(pair[t], up[t, pl.ds(p * 384, 384), :]) for t in range(5))

    def step(k):
        zr[-1].wait_recv()
        if k < 4:
            zr.append(push(pa(z - k, y), ZP))
        yr[-k] = push(pa(z - k, y), YP)
        yl[-k] = push(pa(z - k, y), YM)
        if k < 4:
            zl[-1].wait_recv()
            if k < 3:
                zl.append(push(pa(z + k, y), ZM))
            yr[k] = push(pa(z + k, y), YP)
            yl[k] = push(pa(z + k, y), YM)

    yr2, yl2 = [], []

    def turn(d):
        if d in (0, -1, -2, -3):
            yr[d].wait_recv()
            yr2.append(push(pa(z + d, y - 1), YP))
        else:
            yl[d].wait_recv()
            yl2.append(push(pa(z + d, y + 1), YM))

    l_up.wait()
    gm_send[0] = grad_block(hd).astype(BF16)
    gm_send[1] = grad_block(hs).astype(BF16)
    step(1)
    by[0].wait_recv()
    by2 = push(pb(z, y - 1), YP)
    turn(0)

    x_s.wait_recv()
    x_f.wait_recv()

    def put(sl, v):
        normed[:, sl] = v

    normalize([xbuf[c].astype(F32) for c in range(4)], put)
    l_wq.wait()
    q = nn_dot(normed[...], wq[...])
    for i in range(2):
        qn = (rms(q[:, i * 128 : (i + 1) * 128]) * QSCALE).astype(BF16)
        for p in range(4):
            qall[p, 2 * h + i] = qn[p * 64 : (p + 1) * 64]

    def heads(c):
        return qall.at[:, pl.ds(2 * c, 2)]

    q_x = push(heads(h), XH)
    q_s = push(heads(h), SIB)
    step(2)
    by[1].wait_recv()
    by2.wait_recv()
    bp = [remote(gb(z - i), gb(z - i), ZP) for i in range(3)]
    bm = [remote(gb(z + i), gb(z + i), ZM) for i in range(4)]
    bp[0].start()
    bm[0].start()
    turn(-1)
    turn(1)
    gm_own[0] = grad_block(hx)
    step(3)
    turn(-2)
    turn(2)
    q_x.wait_recv()
    q_f = push(heads(hx), SIB)
    gm_1 = [send(gm_send.at[i], gm_recv.at[i], SIB) for i in range(2)]
    gm_own[1] = grad_block(h)
    step(4)
    turn(-3)
    turn(3)
    acc[...] = jnp.zeros_like(acc)
    q_s.wait_recv()
    q_f.wait_recv()
    gm_2 = remote(gm_send.at[2], gm_recv.at[2], XH)

    def keys_values(i):
        ya = (y + i + i // 2 - 2 * (i // 3)) % 4
        keys, vals = [], []
        for group, n in (
            (kva[pl.ds(ya * 8, 8)], RA),
            (kvb[pl.ds(((z - i + 8) % 8) * 4, 4)], RB),
            (kvb[pl.ds(((z + i + 1) % 8) * 4, 4)], RB),
        ):
            slots = group.shape[0]
            rest = group[:, 4 * n : 5 * n]
            turned = jnp.concatenate([rest[:, :, 64:128], rest[:, :, 0:64]], axis=2)
            rest = jnp.concatenate([rest, turned], axis=1).reshape(slots * 2 * n, 128)
            at_lane = lax.broadcasted_iota(jnp.int32, rest.shape, 1)
            rest = jnp.where(at_lane < 64, rest, (at_lane == 64).astype(BF16))
            keys.append(group[:, 0 : 2 * n].reshape(slots * 2 * n, 128))
            first = group[:, 2 * n : 4 * n].reshape(slots * 2 * n, 128)
            vals.append(jnp.concatenate([first, rest], axis=1))
        return jnp.concatenate(keys, axis=0), jnp.concatenate(vals, axis=0)

    def attend(p, keys, vals):
        w = jnp.exp2(nt_dot(qall[p].reshape(512, 128), keys)).astype(BF16)
        return nn_dot(w, vals)

    yr2_3 = pa(z - 4, y + 1)
    last_l = remote(yr2_3, yr2_3, YM)

    wo_f = [remote(wo.at[hx, r], wo.at[hx, r], SIB) for r in wo_rows]

    @pl.loop(0, 3)
    def _(i):
        @pl.when(i == 0)
        def _():
            bm[0].wait_recv()
            bm[1].start()
            bp[0].wait_recv()
            bp[1].start()

        @pl.when(i == 1)
        def _():
            yl[-4].wait_recv()
            last_l.start()
            for d in (0, -1, -2, -3):
                yl[d].wait_recv()
            bm[1].wait_recv()
            bm[2].start()
            gm_1[0].wait_recv()
            gm_send[2] = (gm_own[0] + gm_recv[0].astype(F32)).astype(BF16)
            gm_2.start()
            wo_x[0].wait_recv()
            wo_f[0].start()

        @pl.when(i == 2)
        def _():
            wo_x[1].wait_recv()
            wo_f[1].start()
            for d in (1, 2, 3, -4):
                yr[d].wait_recv()
            bp[1].wait_recv()
            bp[2].start()
            bm[2].wait_recv()
            bm[3].start()

        keys, vals = keys_values(i)
        for p in range(4):
            acc[p] += attend(p, keys, vals)

    for c in yr2 + yl2 + [last_l, bp[2], bm[3]]:
        c.wait_recv()
    keys, vals = keys_values(3)
    lane = lax.broadcasted_iota(jnp.int32, (512, 256), 1)

    def packed(part):
        den = part[:, 192:193]
        low = den - den.astype(BF16).astype(F32)
        return jnp.where(lane == 193, low, part).astype(BF16)

    o_1 = []
    for i, p in enumerate((hd, hs)):
        o_send[i] = packed(acc[p] + attend(p, keys, vals))
        o_1.append(send(o_send.at[i], o_recv.at[i], SIB))
    for p in (hx, h):
        acc[p] += attend(p, keys, vals)

    def clear(part):
        return jnp.where(lane == 193, 0.0, part)

    def widen(part):
        part = part.astype(F32)
        return jnp.where(lane == 192, part + part[:, 193:194], clear(part))

    o_1[0].wait_recv()
    o_send[2] = packed(clear(acc[hx]) + widen(o_recv[0]))
    o_2 = send(o_send.at[2], o_recv.at[2], XH)

    wo_x[2].wait_recv()
    wo_f[2].start()

    o_1[1].wait_recv()
    tot = clear(acc[h]) + widen(o_recv[1])
    gm_1[1].wait_recv()
    gm_2.wait_recv()
    gm_ref[...] = (gm_own[1] + gm_recv[1].astype(F32) + gm_recv[2].astype(F32)).astype(BF16)
    for c in wo_s + wo_f:
        c.wait_recv()
    o_2.wait_recv()
    tot = tot + widen(o_recv[2])
    att = (tot[:, 0:192] / tot[:, 192:193]).astype(BF16)
    att = jnp.concatenate([att[g * 64 : (g + 1) * 64] for g in range(8)], axis=1)
    pooled = jnp.concatenate([xq[c] for c in range(4)], axis=1).astype(F32)
    m_x, m_s, m_f = [], [], []
    for c in range(3):
        col = slice(c * 512, (c + 1) * 512)
        part = pooled[:, col]
        for b in range(4):
            part = part + nn_dot(att[:, b * 384 : (b + 1) * 384], wo[b, :, col])
        mbuf[c, h] = part.astype(BF16)
        m_x.append(push(mbuf.at[c, h], XH))
        m_s.append(push(mbuf.at[c, h], SIB))
    for c in range(3):
        m_x[c].wait_recv()
        m_f.append(push(mbuf.at[c, hx], SIB))
    c_h = []
    taps = [0.0] * 5
    for c in range(3):
        m_s[c].wait_recv()
        m_f[c].wait_recv()
        c_h.append(send(mbuf.at[c, 3, pl.ds(48, 16)], halo.at[0, c], NXT))
        c_h.append(send(mbuf.at[c, 0, pl.ds(0, 16)], halo.at[1, c], PRV))
        full = mbuf[c].reshape(256, 512)
        for t in range(5):
            taps[t] = taps[t] + nn_dot(full, up[t, c * 512 : (c + 1) * 512, :])

    def edge(side, t):
        return sum(nn_dot(halo[side, c], up[t, c * 512 : (c + 1) * 512, :]) for c in range(3))

    for c in c_h:
        c.wait_recv()
    has_prev = (s > 0).astype(F32)
    has_next = (s < 63).astype(F32)
    lo = [edge(0, t) * has_prev for t in (0, 1)]
    hi = [edge(1, t) * has_next for t in (3, 4)]

    def shifted(v, before, after, which):
        tbuf[which, 0:16, :] = before
        tbuf[which, 16:272, :] = v
        tbuf[which, 272:288, :] = after

    none = jnp.zeros((16, 384), F32)
    shifted(taps[0] + taps[1], lo[0] + lo[1], none, 0)
    shifted(taps[4], none, hi[1], 1)
    shifted(taps[0], lo[0], none, 2)
    shifted(taps[3] + taps[4], none, hi[0] + hi[1], 3)
    even = tbuf[0, 15:271, :] + (taps[2] + taps[3]) + tbuf[1, 17:273, :]
    odd = tbuf[2, 15:271, :] + (taps[1] + taps[2]) + tbuf[3, 17:273, :]
    for c in range(3):
        lanes = slice(c * 128, (c + 1) * 128)
        o32[c, pl.ds(0, 256, stride=2), :] = even[:, lanes]
        o32[c, pl.ds(1, 256, stride=2), :] = odd[:, lanes]
        out_ref[:, lanes] = (o32[c] + lv32[c]).astype(BF16)

    for c in sent:
        c.wait_send()


def per_device(level_input, norm_gain, query_weight, key_weight, value_weight, out_weight, up_weight, grad_output):
    any_spec = pl.BlockSpec(memory_space=pl.ANY)
    vmem = pl.BlockSpec(memory_space=pltpu.VMEM)
    v = pltpu.VMEM
    outs = pl.pallas_call(
        kernel,
        out_shape=(
            jax.ShapeDtypeStruct((512, 384), BF16),
            jax.ShapeDtypeStruct((256, 384), BF16),
        ),
        in_specs=[any_spec] * 8,
        out_specs=(vmem, vmem),
        scratch_shapes=[
            v((512, 384), BF16), v((1536,), F32), v((1536, 256), BF16), v((1536, 128), BF16),
            v((192, 1536), BF16), v((4, 384, 1536), BF16), v((5, 1536, 384), BF16), v((544, 384), BF16),
            v((3, 512, 128), F32), v((3, 544, 128), F32), v((4, 256, 384), BF16), v((4, 64, 384), BF16),
            v((256, 1536), BF16), v((4, 8, 64, 128), BF16), v((2, 64, 384), BF16), v((32, 5 * RA, 128), BF16),
            v((32, 5 * RB, 128), BF16), v((4, 512, 256), F32),
            v((2, 256, 384), F32), v((3, 256, 384), BF16), v((3, 256, 384), BF16),
            v((3, 512, 256), BF16), v((3, 512, 256), BF16),
            v((3, 4, 64, 512), BF16), v((2, 3, 16, 512), BF16), v((4, 288, 384), F32), v((3, 512, 128), F32),
            pltpu.SemaphoreType.DMA((8,)),
            pltpu.SemaphoreType.DMA((N_SEM,)),
            pltpu.SemaphoreType.DMA((N_SEM,)),
        ],
        compiler_params=pltpu.CompilerParams(
            collective_id=0, has_side_effects=True, vmem_limit_bytes=56 << 20
        ),
    )(
        level_input, norm_gain, query_weight, key_weight, value_weight.T,
        out_weight, up_weight, grad_output,
    )
    def emit(a, b, c, d):
        c[...] = a[...]
        d[...] = b[...]

    return pl.pallas_call(
        emit,
        out_shape=tuple(jax.ShapeDtypeStruct(o.shape, o.dtype) for o in outs),
        in_specs=[vmem] * 2,
        out_specs=(vmem, vmem),
    )(*outs)


def solution(mesh):
    in_specs = (
        P("seq", "head"), P(), P(None, "head"), P(), P(), P("head", None),
        P(None, None, "head"), P("seq", "head"),
    )
    out_specs = (P("seq", "head"), P("seq", "head"))
    return jax.shard_map(
        per_device, mesh=mesh, in_specs=in_specs, out_specs=out_specs, check_vma=False
    )
```
